32 devices in a mesh: shots: 2 (over x), depth: 8 (over z, y), freq: 2 (over core).
Axes of the slice: x: 2, y: 2, z: 4, core: 2. Of those that a mesh axis runs over, the one named last changes fastest.
Arguments:
- surface: float32 [2, 4, 2, 128, 256], P('shots', 'freq'), parts along dimension 0, may hold values from -2.1 to 2.1
- bins: int32 [8, 128, 128], P('depth'), may hold values from 0 to 7
- stencil: float32 [4, 8, 5], P('freq'), may hold values from 0.25 to 1
- phase_step: float32 [4, 8], P('freq'), may hold values from 0.3 to 1.4
- phase_shift: float32 [4, 8], P('freq'), may hold values from -3.140625 to 3.140625
- lags: int32 [4], replicated, may hold values from 0 to 7, as said below
Outputs:
- image: float32 [8, 8, 16384], P('depth', 'shots', 'freq'), parts along dimension 1
The draws below stay inside these ranges and needn't reach their ends.
There are 2 independent parts, one for each index of `shots`. The reference program is written for one: setup_inputs(seed, part) draws one part's arguments, and reference() takes and returns one part's arrays. A program takes and returns all parts, laid end to end along the dimension named above; an argument that names none is the same for every part. Nothing has to cross between parts.
Inputs may be any that keep to these rules, and one draw needn't show every extreme that they name: `lags`: 4 distinct half-offsets in cells; one of them is 7.
All inputs are finite; a program needn't handle non-finite values.
Results may differ from the reference program's by a relative error of at most 0.0003.
Values sent between devices are 32-bit elements; how exact they have to be, the bound alone decides.
A program may use at most 64 MiB of HBM per device.

```python
import math
import jax
import jax.numpy as jnp
from jax import lax

G = 128
SHOTS = 1
KERNELS = 8
TAPS = 13
HALF = 6
LAGS = 4
HMAX = 7
NF = 4
NZ = 8


def draw_lags(key, part):
    order = jax.random.permutation(key, HMAX).astype(jnp.int32)
    chosen = jnp.concatenate([order[:LAGS - 1], jnp.array([HMAX], jnp.int32)])
    return jax.random.permutation(jax.random.fold_in(key, 7), chosen).astype(jnp.int32)


def plant(result, stream_key, low, largest):
    shape = result.shape
    spot = [jax.random.randint(jax.random.fold_in(stream_key, axis), (), 0, shape[axis]) for axis in range(len(shape))]
    result = result.at[tuple(spot)].set(low)
    longest = shape.index(max(shape))
    spot[longest] = (spot[longest] + 1) % shape[longest]
    return result.at[tuple(spot)].set(largest)


def block_scale(own_key, extent, pieces, smallest, high):
    def one(position, blocks):
        steps = jax.random.uniform(jax.random.fold_in(jax.random.fold_in(own_key, 6), position), (blocks,), jnp.float32, smallest / len(pieces), high / len(pieces))
        return jnp.repeat(jnp.exp(steps), extent[position] // blocks).reshape((-1,) + (1,) * (len(extent) - position - 1))

    gain = one(*pieces[0])
    for cut in pieces[1:]:
        gain = gain * one(*cut)
    return gain


def bell_draw(key, shape, deviation, most, split=(), kind=jnp.bfloat16):
    entries = deviation * jax.random.normal(key, shape, jnp.float32)
    if split:
        entries = entries * block_scale(key, shape, split, -0.22, 0.18)
    return jnp.clip(entries, -most, most).astype(kind)


def setup_inputs(seed: int = 0, part: int = 0) -> dict:
    key_of = jax.random.split(jax.random.key(seed), 7)
    part_keys = jax.random.split(jax.random.fold_in(key_of[6], part), 7)
    surface = bell_draw(part_keys[0], (SHOTS, NF, 2, G, 2 * G), 0.35, 2.1, ((1, 2),), jnp.float32)
    bins = plant(jax.random.randint(key_of[1], (NZ, G, G), 0, KERNELS), jax.random.fold_in(key_of[1], 1), 0, KERNELS - 1).astype(jnp.int32)
    stencil = jnp.clip(0.25 + 0.75 * jax.random.uniform(key_of[2], (NF, KERNELS, 5), jnp.float32) ** block_scale(key_of[2], (NF, KERNELS, 5), ((0, 2),), -0.2, 0.2), 0.25, 1.0)
    phase_step = jnp.clip(jnp.exp(math.log(1.4) - 1.540445 * jax.random.uniform(key_of[3], (NF, KERNELS), jnp.float32) ** block_scale(key_of[3], (NF, KERNELS), ((0, 2),), -0.2, 0.2)), 0.3, 1.4)
    phase_shift = jnp.clip(jax.random.uniform(key_of[4], (NF, KERNELS), jnp.float32, -3.140625, 3.140625), -3.140625, 3.140625)
    lags = draw_lags(jax.random.fold_in(key_of[6], 71), part)
    return dict(surface=surface, bins=bins, stencil=stencil, phase_step=phase_step, phase_shift=phase_shift, lags=lags)


def kernel_taps(stencil, phase_step, phase_shift):
    center = stencil[..., 0]
    along_x = stencil[..., 1]
    along_y = stencil[..., 2]
    diag_main = stencil[..., 3]
    diag_anti = stencil[..., 4]
    row_above = jnp.stack([diag_main, along_y, diag_anti], -1)
    row_middle = jnp.stack([along_x, center, along_x], -1)
    row_below = jnp.stack([diag_anti, along_y, diag_main], -1)
    stencil_grid = jnp.stack([row_above, row_middle, row_below], -2)
    weight_sum = center + 2.0 * (along_x + along_y + diag_main + diag_anti)
    stencil_grid = stencil_grid * (phase_step / weight_sum)[..., None, None]
    lead = stencil.shape[:-1]
    tap_rows = lax.broadcasted_iota(jnp.int32, (TAPS, TAPS), 0)
    tap_cols = lax.broadcasted_iota(jnp.int32, (TAPS, TAPS), 1)
    unit_tap = ((tap_rows == HALF) & (tap_cols == HALF)).astype(jnp.float32)
    power = jnp.broadcast_to(unit_tap, lead + (TAPS, TAPS)).astype(jnp.float32)
    real_sum = power
    imag_sum = jnp.zeros(lead + (TAPS, TAPS), jnp.float32)
    pad_spec = [(0, 0)] * len(lead) + [(1, 1), (1, 1)]
    for order in range(1, HALF + 1):
        padded = jnp.pad(power, pad_spec)
        grown = jnp.zeros(lead + (TAPS, TAPS), jnp.float32)
        for row_off in range(3):
            for col_off in range(3):
                piece = padded[..., 2 - row_off:2 - row_off + TAPS, 2 - col_off:2 - col_off + TAPS]
                grown = grown + stencil_grid[..., row_off, col_off, None, None] * piece
        power = grown
        weighted = power * (1.0 / math.factorial(order))
        if order % 4 == 1:
            imag_sum = imag_sum + weighted
        elif order % 4 == 2:
            real_sum = real_sum - weighted
        elif order % 4 == 3:
            imag_sum = imag_sum - weighted
        else:
            real_sum = real_sum + weighted
    cosine = jnp.cos(phase_shift)[..., None, None]
    sine = jnp.sin(phase_shift)[..., None, None]
    return cosine * real_sum - sine * imag_sum, sine * real_sum + cosine * imag_sum


def reference(surface, bins, stencil, phase_step, phase_shift, lags):
    kern_real, kern_imag = kernel_taps(stencil, phase_step, phase_shift)
    padded_size = G + 2 * HALF
    kernel = kern_real + 1j * kern_imag
    flipped = kernel[..., ::-1, ::-1]
    placed = jnp.pad(flipped, ((0, 0), (0, 0), (0, padded_size - TAPS), (0, padded_size - TAPS)))
    placed = jnp.roll(placed, (-HALF, -HALF), axis=(2, 3))
    spectrum = jnp.fft.fft2(placed)
    wavefield = surface[..., :G] + 1j * surface[..., G:]
    kernel_ids = jnp.arange(KERNELS).astype(jnp.int32)

    def descend(fields, level_bins):
        padded = jnp.pad(fields, ((0, 0), (0, 0), (0, 0), (0, padded_size - G), (0, padded_size - G)))
        field_spec = jnp.fft.fft2(padded)
        convolved = jnp.fft.ifft2(field_spec[:, :, :, None] * spectrum[None, :, None])[..., :G, :G]
        selector = (level_bins[None] == kernel_ids[:, None, None]).astype(jnp.float32)
        fields = jnp.sum(convolved * selector, axis=3)
        source_pad = jnp.pad(fields[:, :, 0], ((0, 0), (0, 0), (0, 0), (HMAX, HMAX)))
        receiver_pad = jnp.pad(fields[:, :, 1], ((0, 0), (0, 0), (0, 0), (HMAX, HMAX)))
        lag_terms = []
        for lag_index in range(LAGS):
            offset = lags[lag_index].astype(jnp.int32)
            shifted_source = lax.dynamic_slice_in_dim(source_pad, (HMAX - offset).astype(jnp.int32), G, 3)
            shifted_receiver = lax.dynamic_slice_in_dim(receiver_pad, (HMAX + offset).astype(jnp.int32), G, 3)
            product = jnp.real(jnp.conj(shifted_source) * shifted_receiver)
            lag_terms.append(jnp.sum(product, axis=(0, 1)).reshape(G * G))
        return fields, jnp.stack(lag_terms)

    unused, image = lax.scan(descend, wavefield, bins)
    return image
```

```python
import functools
import math

import jax
import jax.numpy as jnp
from jax import lax
from jax.experimental import pallas as pl
from jax.experimental.pallas import tpu as pltpu
from jax.sharding import PartitionSpec as P

HALF = 6
TAPS = 2 * HALF + 1
HALO = 8
ROWS = 16
WINDOW = ROWS + 2 * HALO
PARTS = 4
LANES = 128
PER_TILE = LANES // WINDOW
MAIN = (TAPS // PER_TILE) * LANES
CONTRACT = 3 * MAIN + LANES
MESH = pl.DeviceIdType.MESH


def snake(index):
    pair = index // 2
    return 2 * pair + (index % 2 + pair % 2) % 2


def column(row_values, count):
    rows = lax.broadcasted_iota(jnp.int32, (count, count), 0)
    cols = lax.broadcasted_iota(jnp.int32, (count, count), 1)
    spread = jnp.broadcast_to(row_values, (count, count))
    return jnp.sum(jnp.where(rows == cols, spread, 0.0), axis=1, keepdims=True)


def build_taps(weights, step, shift, kernels):
    center, along_x, along_y, main, anti = (weights[:, j : j + 1] for j in range(5))
    scale = step / (center + 2.0 * (along_x + along_y + main + anti))
    center, along_x, along_y, main, anti = (
        jnp.broadcast_to(part * scale, (kernels, LANES))
        for part in (center, along_x, along_y, main, anti)
    )
    lane = lax.broadcasted_iota(jnp.int32, (kernels, LANES), 1)
    tiles = -(-TAPS // PER_TILE)
    zero = jnp.zeros((kernels, LANES), jnp.float32)
    power = [zero for _ in range(tiles)]
    spot = (HALF % PER_TILE) * WINDOW + HALO
    power[HALF // PER_TILE] = jnp.where(lane == spot, 1.0, 0.0)
    real = list(power)
    imag = [zero for _ in range(tiles)]
    for order in range(1, HALF + 1):
        right = [pltpu.roll(tile, WINDOW, 1) for tile in power]
        left = [pltpu.roll(tile, LANES - WINDOW, 1) for tile in power]
        grown = []
        for t in range(tiles):
            before = jnp.where(lane < WINDOW, right[t - 1] if t else zero, right[t])
            after = jnp.where(
                lane >= LANES - WINDOW, left[t + 1] if t + 1 < tiles else zero, left[t]
            )
            tall = along_y * power[t]
            down = tall + main * before + anti * after
            up = tall + main * after + anti * before
            flat = center * power[t] + along_x * (before + after)
            grown.append(flat + pltpu.roll(down, 1, 1) + pltpu.roll(up, LANES - 1, 1))
        power = grown
        sign = 1.0 if order % 4 < 2 else -1.0
        factor = sign / math.factorial(order)
        target = imag if order % 2 else real
        for t in range(tiles):
            target[t] = target[t] + power[t] * factor
    cosine = jnp.broadcast_to(jnp.cos(shift), (kernels, LANES))
    sine = jnp.broadcast_to(jnp.sin(shift), (kernels, LANES))
    kern_real = [cosine * r - sine * i for r, i in zip(real, imag)]
    kern_imag = [sine * r + cosine * i for r, i in zip(real, imag)]
    return kern_real, kern_imag


def split(value):
    high = value.astype(jnp.bfloat16)
    low = (value - high.astype(jnp.float32)).astype(jnp.bfloat16)
    return high, low


def kernel(
    depth, groups, freqs,
    surface, bins, stencil, phase_step, phase_shift, lags, out,
    field, level_bins, spread, taps, patches, part, mirror, total,
    bins_send, bins_recv, halo_send, halo_recv, swap_send, swap_recv, out_send, out_recv,
):
    freq_count = surface.shape[1]
    kernels = stencil.shape[1]
    width = surface.shape[4] // 2
    lag_count = lags.shape[0]
    strips = depth // groups
    share = lag_count // freqs
    per_core = strips // freqs
    here = lax.axis_index("depth")
    core = lax.axis_index("freq")
    group = here // strips
    strip = snake(here % strips)
    has_up = strip > 0
    has_down = strip < strips - 1

    field[...] = jnp.zeros_like(field)
    first = pl.multiple_of(strip * ROWS, ROWS)
    for f in range(freq_count):
        for j in range(PARTS):
            cols = pl.ds((j % 2) * width, width)
            field[0, f, j, pl.ds(HALO, ROWS), :] = surface[0, f, j // 2, pl.ds(first, ROWS), cols]

            @pl.when(has_up)
            def _():
                above = pl.multiple_of(jnp.maximum(first - HALO, 0), HALO)
                field[0, f, j, pl.ds(0, HALO), :] = surface[0, f, j // 2, pl.ds(above, HALO), cols]

            @pl.when(has_down)
            def _():
                below = pl.multiple_of(jnp.minimum(first + ROWS, (strips - 1) * ROWS), HALO)
                field[0, f, j, pl.ds(HALO + ROWS, HALO), :] = surface[
                    0, f, j // 2, pl.ds(below, HALO), cols
                ]

    barrier = pltpu.get_barrier_semaphore()

    def greet(step, carry):
        other = (here * freqs + core + step) % (depth * freqs)
        pl.semaphore_signal(
            barrier, inc=1, device_id={"depth": other // freqs, "freq": other % freqs},
            device_id_type=MESH,
        )
        return carry

    lax.fori_loop(1, depth * freqs, greet, 0)

    level_bins[here] = bins[0, pl.ds(first, ROWS), :]
    for f in range(freq_count):
        patches[f, 3 * MAIN + 3 * WINDOW :, :] = jnp.zeros((WINDOW, PARTS * width), jnp.bfloat16)
        step = column(phase_step[f : f + 1, :], kernels)
        shift = column(phase_shift[f : f + 1, :], kernels)
        kern = build_taps(stencil[f], step, shift, kernels)
        for c in range(2):
            for t in range(len(kern[c])):
                for y in range(ROWS):
                    moved = pltpu.roll(kern[c][t], y, 1) if y else kern[c][t]
                    spread[f, t, pl.ds(c * ROWS + y, kernels, stride=2 * ROWS), :] = moved
        for t in range(MAIN // LANES):
            high, low = split(spread[f, t])
            taps[f, :, t * LANES : (t + 1) * LANES] = high
            taps[f, :, MAIN + t * LANES : MAIN + (t + 1) * LANES] = high
            taps[f, :, 2 * MAIN + t * LANES : 2 * MAIN + (t + 1) * LANES] = low
        high, low = split(spread[f, MAIN // LANES])
        high, low = high.astype(jnp.float32), low.astype(jnp.float32)
        last = high + pltpu.roll(high, WINDOW, 1) + pltpu.roll(low, 2 * WINDOW, 1)
        taps[f, :, 3 * MAIN :] = last.astype(jnp.bfloat16)

    pl.semaphore_wait(barrier, depth * freqs - 1)

    def bins_copy(target, level, sem):
        rows = pl.ds(pl.multiple_of(snake(target % strips) * ROWS, ROWS), ROWS)
        return pltpu.make_async_remote_copy(
            src_ref=bins.at[0, rows, :], dst_ref=level_bins.at[level],
            send_sem=bins_send.at[sem], recv_sem=bins_recv.at[level],
            device_id={"depth": target}, device_id_type=MESH,
        )

    def send_bins(step, carry):
        bins_copy((here + step) % depth, here, step).start()
        return carry

    lax.fori_loop(1, depth, send_bins, 0)

    up = group * strips + snake(jnp.maximum(strip - 1, 0))
    down = group * strips + snake(jnp.minimum(strip + 1, strips - 1))

    def halo_copy(slot, f, way):
        source = HALO if way == 0 else ROWS
        target = HALO + ROWS if way == 0 else 0
        return pltpu.make_async_remote_copy(
            src_ref=field.at[slot, f, :, pl.ds(source, HALO), :],
            dst_ref=field.at[slot, f, :, pl.ds(target, HALO), :],
            send_sem=halo_send.at[way, slot, f], recv_sem=halo_recv.at[way, slot, f],
            device_id={"depth": up if way == 0 else down}, device_id_type=MESH,
        )

    def swap_copy(index):
        return pltpu.make_async_remote_copy(
            src_ref=part.at[index, pl.ds((1 - core) * share, share)], dst_ref=mirror.at[index],
            send_sem=swap_send.at[index], recv_sem=swap_recv.at[index],
            device_id={"freq": 1 - core}, device_id_type=MESH,
        )

    out_core = strip // per_core

    def out_copy(index, from_core, from_place):
        rows = pl.ds(pl.multiple_of(from_place * ROWS, ROWS), ROWS)
        return pltpu.make_async_remote_copy(
            src_ref=total.at[index], dst_ref=out.at[pl.ds(from_core * share, share), rows, :],
            send_sem=out_send.at[index], recv_sem=out_recv.at[from_core, from_place],
            device_id={"depth": group * strips + index, "freq": out_core}, device_id_type=MESH,
        )

    def owned(index):
        return (group * strips + index == here) & (out_core == core)

    def deliver(index):
        swap_copy(index).wait()
        mine = part[index, pl.ds(core * share, share)] + mirror[index]

        @pl.when(owned(index))
        def _():
            rows = pl.ds(pl.multiple_of(strip % per_core * ROWS, ROWS), ROWS)
            out[pl.ds(core * share, share), rows, :] = mine

        @pl.when(jnp.logical_not(owned(index)))
        def _():
            total[index] = mine
            out_copy(index, core, strip % per_core).start()

    wide = lax.broadcasted_iota(jnp.int32, (WINDOW, width), 1)
    lane = lax.broadcasted_iota(jnp.int32, (ROWS, width), 1)

    def level(z, carry):
        slot = z % 2
        after = 1 - slot

        for f in range(freq_count):
            for way, has_send, has_recv in ((0, has_up, has_down), (1, has_down, has_up)):

                @pl.when((z > 0) & has_recv)
                def _():
                    halo_copy(slot, f, way).wait_recv()

                @pl.when((z > 0) & has_send)
                def _():
                    halo_copy(slot, f, way).wait_send()

            for j in range(PARTS):
                values = field[slot, f, j]
                cols = slice(j * width, (j + 1) * width)
                for b in range(TAPS):
                    reach = b - HALF
                    moved = values
                    if reach:
                        moved = pltpu.roll(values, (-reach) % width, 1)
                        inside = wide < width - reach if reach > 0 else wide >= -reach
                        moved = jnp.where(inside, moved, 0.0)
                    high, low = split(moved)
                    if b < TAPS - 1:
                        places = [b * WINDOW + n * MAIN for n in range(3)]
                    else:
                        places = [3 * MAIN + n * WINDOW for n in range(3)]
                    for place, piece in zip(places, (high, low, high)):
                        patches[f, place : place + WINDOW, cols] = piece
            result = jnp.dot(taps[f], patches[f], preferred_element_type=jnp.float32)

            if f == 0:

                @pl.when(z != here)
                def _():
                    bins_copy(here, z, 0).wait_recv()

            chosen = level_bins[z]
            picked = None
            for k in range(kernels):
                rows = [
                    [
                        result[
                            (2 * k + c) * ROWS : (2 * k + c + 1) * ROWS,
                            j * width : (j + 1) * width,
                        ]
                        for j in range(PARTS)
                    ]
                    for c in range(2)
                ]
                if picked is None:
                    picked = rows
                else:
                    mask = chosen == k
                    picked = [
                        [jnp.where(mask, rows[c][j], picked[c][j]) for j in range(PARTS)]
                        for c in range(2)
                    ]
            for pair in range(PARTS // 2):
                re, im = 2 * pair, 2 * pair + 1
                field[after, f, re, pl.ds(HALO, ROWS), :] = picked[0][re] - picked[1][im]
                field[after, f, im, pl.ds(HALO, ROWS), :] = picked[0][im] + picked[1][re]

            for way, has_send in ((0, has_up), (1, has_down)):

                @pl.when((z < depth - 1) & has_send)
                def _():
                    halo_copy(after, f, way).start()

        index = z - group * strips

        @pl.when((index >= 0) & (index < strips))
        def _():
            for n in range(lag_count):
                lag = lags[n]
                back = lax.rem(width - 2 * lag, width)
                product = jnp.zeros((ROWS, width), jnp.float32)
                for f in range(freq_count):
                    for j in range(PARTS // 2):
                        source = field[after, f, j, pl.ds(HALO, ROWS), :]
                        receiver = field[after, f, 2 + j, pl.ds(HALO, ROWS), :]
                        product += source * pltpu.roll(receiver, back, 1)
                product = jnp.where(lane < width - 2 * lag, product, 0.0)
                part[index, n] = pltpu.roll(product, lag, 1)
            swap_copy(index).start()

        @pl.when((index >= 1) & (index <= strips))
        def _():
            deliver(index - 1)

        return carry

    lax.fori_loop(0, depth, level, 0)

    @pl.when(group == groups - 1)
    def _():
        deliver(strips - 1)

    def finish_out(index, carry):
        @pl.when(jnp.logical_not(owned(index)))
        def _():
            out_copy(index, core, strip % per_core).wait_send()

        return carry

    def finish_bins(step, carry):
        bins_copy((here + step) % depth, here, step).wait_send()
        return carry

    for from_core in range(freqs):
        for place in range(per_core):
            sender = core * per_core + place

            @pl.when((sender != strip) | (core != from_core))
            def _():
                out_copy(0, from_core, place).wait_recv()

    lax.fori_loop(0, strips, finish_out, 0)
    lax.fori_loop(1, depth, finish_bins, 0)


def body(surface, bins, stencil, phase_step, phase_shift, lags, *, depth, freqs):
    freq_count = surface.shape[1]
    height = surface.shape[3]
    width = surface.shape[4] // 2
    kernels = stencil.shape[1]
    lag_count = lags.shape[0]
    strips = height // ROWS
    groups = depth // strips
    per_core = strips // freqs
    share = lag_count // freqs
    tiles = -(-TAPS // PER_TILE)
    cost = 2 * freq_count * depth * 2 * kernels * ROWS * CONTRACT * PARTS * width
    vmem = pl.BlockSpec(memory_space=pltpu.VMEM)
    image = pl.pallas_call(
        functools.partial(kernel, depth, groups, freqs),
        out_shape=jax.ShapeDtypeStruct((lag_count, per_core * ROWS, width), jnp.float32),
        in_specs=[vmem] * 5 + [pl.BlockSpec(memory_space=pltpu.SMEM)],
        out_specs=vmem,
        scratch_shapes=[
            pltpu.VMEM((2, freq_count, PARTS, WINDOW, width), jnp.float32),
            pltpu.VMEM((depth, ROWS, width), jnp.int32),
            pltpu.VMEM((freq_count, tiles, 2 * kernels * ROWS, LANES), jnp.float32),
            pltpu.VMEM((freq_count, 2 * kernels * ROWS, CONTRACT), jnp.bfloat16),
            pltpu.VMEM((freq_count, CONTRACT, PARTS * width), jnp.bfloat16),
            pltpu.VMEM((strips, lag_count, ROWS, width), jnp.float32),
            pltpu.VMEM((strips, share, ROWS, width), jnp.float32),
            pltpu.VMEM((strips, share, ROWS, width), jnp.float32),
            pltpu.SemaphoreType.DMA((depth,)),
            pltpu.SemaphoreType.DMA((depth,)),
            pltpu.SemaphoreType.DMA((2, 2, freq_count)),
            pltpu.SemaphoreType.DMA((2, 2, freq_count)),
            pltpu.SemaphoreType.DMA((strips,)),
            pltpu.SemaphoreType.DMA((strips,)),
            pltpu.SemaphoreType.DMA((strips,)),
            pltpu.SemaphoreType.DMA((freqs, per_core)),
        ],
        compiler_params=pltpu.CompilerParams(
            collective_id=0, has_side_effects=True, vmem_limit_bytes=32 * 1024 * 1024
        ),
        cost_estimate=pl.CostEstimate(flops=cost, bytes_accessed=1 << 20, transcendentals=0),
    )(surface, bins, stencil, phase_step, phase_shift, lags)
    return image.reshape(1, lag_count, per_core * ROWS * width)


def solution(mesh):
    return jax.shard_map(
        functools.partial(body, depth=mesh.shape["depth"], freqs=mesh.shape["freq"]),
        mesh=mesh,
        in_specs=(
            P("shots", "freq", None, None, None),
            P("depth", None, None),
            P("freq", None, None),
            P("freq", None),
            P("freq", None),
            P(),
        ),
        out_specs=P("depth", "shots", "freq"),
        check_vma=False,
    )
```

```python
import functools
import math

import jax
import jax.numpy as jnp
from jax import lax
from jax.experimental import pallas as pl
from jax.experimental.pallas import tpu as pltpu
from jax.sharding import PartitionSpec as P

HALF = 6
TAPS = 2 * HALF + 1
HALO = 8
ROWS = 16
WINDOW = ROWS + 2 * HALO
PARTS = 4
LANES = 128
PER_TILE = LANES // WINDOW
MAIN = (TAPS // PER_TILE) * LANES
CONTRACT = 3 * MAIN + LANES
MESH = pl.DeviceIdType.MESH


def snake(index):
    pair = index // 2
    return 2 * pair + (index % 2 + pair % 2) % 2


def column(row_values, count):
    rows = lax.broadcasted_iota(jnp.int32, (count, count), 0)
    cols = lax.broadcasted_iota(jnp.int32, (count, count), 1)
    spread = jnp.broadcast_to(row_values, (count, count))
    return jnp.sum(jnp.where(rows == cols, spread, 0.0), axis=1, keepdims=True)


def build_taps(weights, step, shift, kernels):
    center, along_x, along_y, main, anti = weights
    scale = step / (center + 2.0 * (along_x + along_y + main + anti))
    center, along_x, along_y, main, anti = (
        jnp.broadcast_to(part * scale, (kernels, LANES))
        for part in (center, along_x, along_y, main, anti)
    )
    lane = lax.broadcasted_iota(jnp.int32, (kernels, LANES), 1)
    tiles = -(-TAPS // PER_TILE)
    zero = jnp.zeros((kernels, LANES), jnp.float32)
    power = [zero for _ in range(tiles)]
    spot = (HALF % PER_TILE) * WINDOW + HALO
    power[HALF // PER_TILE] = jnp.where(lane == spot, 1.0, 0.0)
    real = list(power)
    imag = [zero for _ in range(tiles)]
    for order in range(1, HALF + 1):
        right = [pltpu.roll(tile, WINDOW, 1) for tile in power]
        left = [pltpu.roll(tile, LANES - WINDOW, 1) for tile in power]
        grown = []
        for t in range(tiles):
            before = jnp.where(lane < WINDOW, right[t - 1] if t else zero, right[t])
            after = jnp.where(
                lane >= LANES - WINDOW, left[t + 1] if t + 1 < tiles else zero, left[t]
            )
            tall = along_y * power[t]
            down = tall + main * before + anti * after
            up = tall + main * after + anti * before
            flat = center * power[t] + along_x * (before + after)
            grown.append(flat + pltpu.roll(down, 1, 1) + pltpu.roll(up, LANES - 1, 1))
        power = grown
        sign = 1.0 if order % 4 < 2 else -1.0
        factor = sign / math.factorial(order)
        target = imag if order % 2 else real
        for t in range(tiles):
            target[t] = target[t] + power[t] * factor
    cosine = jnp.broadcast_to(jnp.cos(shift), (kernels, LANES))
    sine = jnp.broadcast_to(jnp.sin(shift), (kernels, LANES))
    kern_real = [cosine * r - sine * i for r, i in zip(real, imag)]
    kern_imag = [sine * r + cosine * i for r, i in zip(real, imag)]
    return kern_real, kern_imag


def split(value):
    high = value.astype(jnp.bfloat16)
    low = (value - high.astype(jnp.float32)).astype(jnp.bfloat16)
    return high, low


def kernel(
    depth, groups, freqs,
    surface, bins, stencil, phase_step, phase_shift, lags, out,
    field, level_bins, spread, taps, patches, part, mirror, total,
    load_sem, bins_send, bins_recv, halo_send, halo_recv, swap_send, swap_recv, out_send, out_recv,
):
    freq_count = surface.shape[1]
    kernels = stencil.shape[2]
    width = surface.shape[4] // 2
    lag_count = lags.shape[0]
    strips = depth // groups
    share = lag_count // freqs
    per_core = strips // freqs
    here = lax.axis_index("depth")
    core = lax.axis_index("freq")
    group = here // strips
    strip = snake(here % strips)
    has_up = strip > 0
    has_down = strip < strips - 1

    field[...] = jnp.zeros_like(field)
    first = pl.multiple_of(strip * ROWS, ROWS)

    def load_copy(c, place):
        rows = (first, jnp.maximum(first - HALO, 0), jnp.minimum(first + ROWS, strips * ROWS - HALO))
        size = (ROWS, HALO, HALO)[place]
        target = (HALO, 0, HALO + ROWS)[place]
        return pltpu.make_async_copy(
            surface.at[0, :, :, pl.ds(pl.multiple_of(rows[place], HALO), size), pl.ds(c * width, width)],
            field.at[0, :, :, c, pl.ds(target, size), :],
            load_sem.at[c, place],
        )

    own_bins = pltpu.make_async_copy(bins.at[0, pl.ds(first, ROWS), :], level_bins.at[here], bins_send.at[0])
    own_bins.start()
    for c in range(2):
        load_copy(c, 0).start()
        pl.when(has_up)(load_copy(c, 1).start)
        pl.when(has_down)(load_copy(c, 2).start)

    barrier = pltpu.get_barrier_semaphore()

    def greet(step, carry):
        other = (here * freqs + core + step) % (depth * freqs)
        pl.semaphore_signal(
            barrier, inc=1, device_id={"depth": other // freqs, "freq": other % freqs},
            device_id_type=MESH,
        )
        return carry

    lax.fori_loop(1, depth * freqs, greet, 0)

    for f in range(freq_count):
        patches[f, 3 * MAIN + 3 * WINDOW :, :] = jnp.zeros((WINDOW, PARTS * width), jnp.bfloat16)
        step = column(phase_step[f : f + 1, :], kernels)
        shift = column(phase_shift[f : f + 1, :], kernels)
        weights = [column(stencil[j, f : f + 1, :], kernels) for j in range(5)]
        kern = build_taps(weights, step, shift, kernels)
        for c in range(2):
            for t in range(len(kern[c])):
                for y in range(ROWS):
                    moved = pltpu.roll(kern[c][t], y, 1) if y else kern[c][t]
                    spread[f, t, pl.ds(c * ROWS + y, kernels, stride=2 * ROWS), :] = moved
        for t in range(MAIN // LANES):
            high, low = split(spread[f, t])
            taps[f, :, t * LANES : (t + 1) * LANES] = high
            taps[f, :, MAIN + t * LANES : MAIN + (t + 1) * LANES] = high
            taps[f, :, 2 * MAIN + t * LANES : 2 * MAIN + (t + 1) * LANES] = low
        high, low = split(spread[f, MAIN // LANES])
        high, low = high.astype(jnp.float32), low.astype(jnp.float32)
        last = high + pltpu.roll(high, WINDOW, 1) + pltpu.roll(low, 2 * WINDOW, 1)
        taps[f, :, 3 * MAIN :] = last.astype(jnp.bfloat16)

    own_bins.wait()
    for c in range(2):
        load_copy(c, 0).wait()
        pl.when(has_up)(load_copy(c, 1).wait)
        pl.when(has_down)(load_copy(c, 2).wait)
    pl.semaphore_wait(barrier, depth * freqs - 1)

    def bins_copy(target, level, sem):
        rows = pl.ds(pl.multiple_of(snake(target % strips) * ROWS, ROWS), ROWS)
        return pltpu.make_async_remote_copy(
            src_ref=bins.at[0, rows, :], dst_ref=level_bins.at[level],
            send_sem=bins_send.at[sem], recv_sem=bins_recv.at[level],
            device_id={"depth": target}, device_id_type=MESH,
        )

    def send_bins(step, carry):
        bins_copy((here + step) % depth, here, step).start()
        return carry

    lax.fori_loop(1, depth, send_bins, 0)

    up = group * strips + snake(jnp.maximum(strip - 1, 0))
    down = group * strips + snake(jnp.minimum(strip + 1, strips - 1))

    def halo_copy(slot, f, way):
        source = HALO if way == 0 else ROWS
        target = HALO + ROWS if way == 0 else 0
        return pltpu.make_async_remote_copy(
            src_ref=field.at[slot, f, :, :, pl.ds(source, HALO), :],
            dst_ref=field.at[slot, f, :, :, pl.ds(target, HALO), :],
            send_sem=halo_send.at[way, slot, f], recv_sem=halo_recv.at[way, slot, f],
            device_id={"depth": up if way == 0 else down}, device_id_type=MESH,
        )

    def swap_copy(index):
        return pltpu.make_async_remote_copy(
            src_ref=part.at[index, pl.ds((1 - core) * share, share)], dst_ref=mirror.at[index],
            send_sem=swap_send.at[index], recv_sem=swap_recv.at[index],
            device_id={"freq": 1 - core}, device_id_type=MESH,
        )

    out_core = strip // per_core

    def out_copy(index, from_core, from_place):
        rows = pl.ds(pl.multiple_of(from_place * ROWS, ROWS), ROWS)
        return pltpu.make_async_remote_copy(
            src_ref=total.at[index], dst_ref=out.at[pl.ds(from_core * share, share), rows, :],
            send_sem=out_send.at[index], recv_sem=out_recv.at[from_core, from_place],
            device_id={"depth": group * strips + index, "freq": out_core}, device_id_type=MESH,
        )

    def owned(index):
        return (group * strips + index == here) & (out_core == core)

    def collect(index):
        swap_copy(index).wait()
        total[index] = part[index, pl.ds(core * share, share)] + mirror[index]

    def deliver(index):
        @pl.when(owned(index))
        def _():
            rows = pl.ds(pl.multiple_of(strip % per_core * ROWS, ROWS), ROWS)
            out[pl.ds(core * share, share), rows, :] = total[index]

        @pl.when(jnp.logical_not(owned(index)))
        def _():
            out_copy(index, core, strip % per_core).start()

    def deliver_early(step, carry):
        index = (strip + step) % strips
        pl.when(index < strips - 1)(lambda: deliver(index))
        return carry

    wide = lax.broadcasted_iota(jnp.int32, (WINDOW, width), 1)
    lane = lax.broadcasted_iota(jnp.int32, (ROWS, width), 1)

    def level(z, carry):
        slot = z % 2
        after = 1 - slot
        index = z - group * strips

        for f in range(freq_count):
            for way, has_send, has_recv in ((0, has_up, has_down), (1, has_down, has_up)):

                @pl.when((z > 0) & has_recv)
                def _():
                    halo_copy(slot, f, way).wait_recv()

                @pl.when((z > 0) & has_send)
                def _():
                    halo_copy(slot, f, way).wait_send()

            if f == freq_count - 1:
                pl.when((index >= 1) & (index <= strips))(lambda: collect(index - 1))

                @pl.when(index == strips - 1)
                def _():
                    lax.fori_loop(1, strips + 1, deliver_early, 0)

                pl.when(index == strips)(lambda: deliver(strips - 1))

            for j in range(PARTS):
                values = field[slot, f, j // 2, j % 2]
                cols = slice(j * width, (j + 1) * width)
                for b in range(TAPS):
                    reach = b - HALF
                    moved = values
                    if reach:
                        moved = pltpu.roll(values, (-reach) % width, 1)
                        inside = wide < width - reach if reach > 0 else wide >= -reach
                        moved = jnp.where(inside, moved, 0.0)
                    high, low = split(moved)
                    if b < TAPS - 1:
                        places = [b * WINDOW + n * MAIN for n in range(3)]
                    else:
                        places = [3 * MAIN + n * WINDOW for n in range(3)]
                    for place, piece in zip(places, (high, low, high)):
                        patches[f, place : place + WINDOW, cols] = piece
            result = jnp.dot(taps[f], patches[f], preferred_element_type=jnp.float32)

            if f == 0:

                @pl.when(z != here)
                def _():
                    bins_copy(here, z, 0).wait_recv()

            chosen = level_bins[z]
            picked = None
            for k in range(kernels):
                rows = [
                    [
                        result[
                            (2 * k + c) * ROWS : (2 * k + c + 1) * ROWS,
                            j * width : (j + 1) * width,
                        ]
                        for j in range(PARTS)
                    ]
                    for c in range(2)
                ]
                if picked is None:
                    picked = rows
                else:
                    mask = chosen == k
                    picked = [
                        [jnp.where(mask, rows[c][j], picked[c][j]) for j in range(PARTS)]
                        for c in range(2)
                    ]
            for pair in range(PARTS // 2):
                re, im = 2 * pair, 2 * pair + 1
                field[after, f, pair, 0, pl.ds(HALO, ROWS), :] = picked[0][re] - picked[1][im]
                field[after, f, pair, 1, pl.ds(HALO, ROWS), :] = picked[0][im] + picked[1][re]

            for way, has_send in ((0, has_up), (1, has_down)):

                @pl.when((z < depth - 1) & has_send)
                def _():
                    halo_copy(after, f, way).start()

        @pl.when((index >= 0) & (index < strips))
        def _():
            for n in range(lag_count):
                lag = lags[n]
                back = lax.rem(width - 2 * lag, width)
                product = jnp.zeros((ROWS, width), jnp.float32)
                for f in range(freq_count):
                    for j in range(PARTS // 2):
                        source = field[after, f, 0, j, pl.ds(HALO, ROWS), :]
                        receiver = field[after, f, 1, j, pl.ds(HALO, ROWS), :]
                        product += source * pltpu.roll(receiver, back, 1)
                product = jnp.where(lane < width - 2 * lag, product, 0.0)
                part[index, n] = pltpu.roll(product, lag, 1)
            swap_copy(index).start()

        return carry

    lax.fori_loop(0, depth, level, 0)

    @pl.when(group == groups - 1)
    def _():
        collect(strips - 1)
        deliver(strips - 1)

    def finish_out(index, carry):
        @pl.when(jnp.logical_not(owned(index)))
        def _():
            out_copy(index, core, strip % per_core).wait_send()

        return carry

    def finish_bins(step, carry):
        bins_copy((here + step) % depth, here, step).wait_send()
        return carry

    for from_core in range(freqs):
        for place in range(per_core):
            sender = core * per_core + place

            @pl.when((sender != strip) | (core != from_core))
            def _():
                out_copy(0, from_core, place).wait_recv()

    lax.fori_loop(0, strips, finish_out, 0)
    lax.fori_loop(1, depth, finish_bins, 0)


def body(surface, bins, stencil, phase_step, phase_shift, lags, *, depth, freqs):
    freq_count = surface.shape[1]
    height = surface.shape[3]
    width = surface.shape[4] // 2
    kernels = stencil.shape[1]
    lag_count = lags.shape[0]
    strips = height // ROWS
    groups = depth // strips
    per_core = strips // freqs
    share = lag_count // freqs
    tiles = -(-TAPS // PER_TILE)
    cost = 2 * freq_count * depth * 2 * kernels * ROWS * CONTRACT * PARTS * width
    vmem = pl.BlockSpec(memory_space=pltpu.VMEM)
    image = pl.pallas_call(
        functools.partial(kernel, depth, groups, freqs),
        out_shape=jax.ShapeDtypeStruct((lag_count, per_core * ROWS, width), jnp.float32),
        in_specs=[pl.BlockSpec(memory_space=pl.ANY)] * 2 + [vmem] * 3 + [pl.BlockSpec(memory_space=pltpu.SMEM)],
        out_specs=vmem,
        scratch_shapes=[
            pltpu.VMEM((2, freq_count, PARTS // 2, 2, WINDOW, width), jnp.float32),
            pltpu.VMEM((depth, ROWS, width), jnp.int32),
            pltpu.VMEM((freq_count, tiles, 2 * kernels * ROWS, LANES), jnp.float32),
            pltpu.VMEM((freq_count, 2 * kernels * ROWS, CONTRACT), jnp.bfloat16),
            pltpu.VMEM((freq_count, CONTRACT, PARTS * width), jnp.bfloat16),
            pltpu.VMEM((strips, lag_count, ROWS, width), jnp.float32),
            pltpu.VMEM((strips, share, ROWS, width), jnp.float32),
            pltpu.VMEM((strips, share, ROWS, width), jnp.float32),
            pltpu.SemaphoreType.DMA((2, 3)),
            pltpu.SemaphoreType.DMA((depth,)),
            pltpu.SemaphoreType.DMA((depth,)),
            pltpu.SemaphoreType.DMA((2, 2, freq_count)),
            pltpu.SemaphoreType.DMA((2, 2, freq_count)),
            pltpu.SemaphoreType.DMA((strips,)),
            pltpu.SemaphoreType.DMA((strips,)),
            pltpu.SemaphoreType.DMA((strips,)),
            pltpu.SemaphoreType.DMA((freqs, per_core)),
        ],
        compiler_params=pltpu.CompilerParams(
            collective_id=0, has_side_effects=True, vmem_limit_bytes=32 * 1024 * 1024
        ),
        cost_estimate=pl.CostEstimate(flops=cost, bytes_accessed=1 << 20, transcendentals=0),
    )(surface, bins, jnp.transpose(stencil, (2, 0, 1)), phase_step, phase_shift, lags)
    return image.reshape(1, lag_count, per_core * ROWS * width)


def solution(mesh):
    return jax.shard_map(
        functools.partial(body, depth=mesh.shape["depth"], freqs=mesh.shape["freq"]),
        mesh=mesh,
        in_specs=(
            P("shots", "freq", None, None, None),
            P("depth", None, None),
            P("freq", None, None),
            P("freq", None),
            P("freq", None),
            P(),
        ),
        out_specs=P("depth", "shots", "freq"),
        check_vma=False,
    )
```

```python
import functools
import math

import jax
import jax.numpy as jnp
from jax import lax
from jax.experimental import pallas as pl
from jax.experimental.pallas import tpu as pltpu
from jax.sharding import PartitionSpec as P

HALF = 6
TAPS = 2 * HALF + 1
HALO = 8
ROWS = 16
WINDOW = ROWS + 2 * HALO
PARTS = 4
LANES = 128
PER_TILE = LANES // WINDOW
MAIN = (TAPS // PER_TILE) * LANES
CONTRACT = 3 * MAIN + LANES
MESH = pl.DeviceIdType.MESH


def snake(index):
    pair = index // 2
    return 2 * pair + (index % 2 + pair % 2) % 2


def column(row_values, count):
    rows = lax.broadcasted_iota(jnp.int32, (count, count), 0)
    cols = lax.broadcasted_iota(jnp.int32, (count, count), 1)
    spread = jnp.broadcast_to(row_values, (count, count))
    return jnp.sum(jnp.where(rows == cols, spread, 0.0), axis=1, keepdims=True)


def build_taps(weights, step, shift, kernels):
    center, along_x, along_y, main, anti = weights
    scale = step / (center + 2.0 * (along_x + along_y + main + anti))
    center, along_x, along_y, main, anti = (
        jnp.broadcast_to(part * scale, (kernels, LANES))
        for part in (center, along_x, along_y, main, anti)
    )
    lane = lax.broadcasted_iota(jnp.int32, (kernels, LANES), 1)
    tiles = -(-TAPS // PER_TILE)
    zero = jnp.zeros((kernels, LANES), jnp.float32)
    power = [zero for _ in range(tiles)]
    spot = (HALF % PER_TILE) * WINDOW + HALO
    power[HALF // PER_TILE] = jnp.where(lane == spot, 1.0, 0.0)
    real = list(power)
    imag = [zero for _ in range(tiles)]
    for order in range(1, HALF + 1):
        right = [pltpu.roll(tile, WINDOW, 1) for tile in power]
        left = [pltpu.roll(tile, LANES - WINDOW, 1) for tile in power]
        grown = []
        for t in range(tiles):
            before = jnp.where(lane < WINDOW, right[t - 1] if t else zero, right[t])
            after = jnp.where(
                lane >= LANES - WINDOW, left[t + 1] if t + 1 < tiles else zero, left[t]
            )
            tall = along_y * power[t]
            down = tall + main * before + anti * after
            up = tall + main * after + anti * before
            flat = center * power[t] + along_x * (before + after)
            grown.append(flat + pltpu.roll(down, 1, 1) + pltpu.roll(up, LANES - 1, 1))
        power = grown
        sign = 1.0 if order % 4 < 2 else -1.0
        factor = sign / math.factorial(order)
        target = imag if order % 2 else real
        for t in range(tiles):
            target[t] = target[t] + power[t] * factor
    cosine = jnp.broadcast_to(jnp.cos(shift), (kernels, LANES))
    sine = jnp.broadcast_to(jnp.sin(shift), (kernels, LANES))
    kern_real = [cosine * r - sine * i for r, i in zip(real, imag)]
    kern_imag = [sine * r + cosine * i for r, i in zip(real, imag)]
    return kern_real, kern_imag


def split(value):
    high = value.astype(jnp.bfloat16)
    low = (value - high.astype(jnp.float32)).astype(jnp.bfloat16)
    return high, low


def kernel(
    depth, groups, freqs,
    surface, bins, stencil_far, phase_step_far, phase_shift_far, lags_far, out,
    stencil, phase_step, phase_shift, lags, small_sem,
    field, level_bins, spread, taps, patches, part, mirror, total,
    load_sem, bins_send, bins_recv, halo_send, halo_recv, swap_send, swap_recv, out_send, out_recv,
):
    freq_count = surface.shape[1]
    kernels = stencil.shape[2]
    width = surface.shape[4] // 2
    lag_count = lags.shape[0]
    strips = depth // groups
    share = lag_count // freqs
    per_core = strips // freqs
    here = lax.axis_index("depth")
    core = lax.axis_index("freq")
    group = here // strips
    strip = snake(here % strips)
    has_up = strip > 0
    has_down = strip < strips - 1

    field[...] = jnp.zeros_like(field)
    first = pl.multiple_of(strip * ROWS, ROWS)

    def load_copy(c, place):
        rows = (first, jnp.maximum(first - HALO, 0), jnp.minimum(first + ROWS, strips * ROWS - HALO))
        size = (ROWS, HALO, HALO)[place]
        target = (HALO, 0, HALO + ROWS)[place]
        return pltpu.make_async_copy(
            surface.at[0, :, :, pl.ds(pl.multiple_of(rows[place], HALO), size), pl.ds(c * width, width)],
            field.at[0, :, :, c, pl.ds(target, size), :],
            load_sem.at[c, place],
        )

    smalls = [
        pltpu.make_async_copy(far, near, small_sem.at[n])
        for n, (far, near) in enumerate((
            (stencil_far, stencil), (phase_step_far, phase_step),
            (phase_shift_far, phase_shift), (lags_far, lags),
        ))
    ]
    for small in smalls:
        small.start()
    own_bins = pltpu.make_async_copy(bins.at[0, pl.ds(first, ROWS), :], level_bins.at[here], bins_send.at[0])
    own_bins.start()
    for c in range(2):
        load_copy(c, 0).start()
        pl.when(has_up)(load_copy(c, 1).start)
        pl.when(has_down)(load_copy(c, 2).start)

    barrier = pltpu.get_barrier_semaphore()

    def greet(step, carry):
        other = (here * freqs + core + step) % (depth * freqs)
        pl.semaphore_signal(
            barrier, inc=1, device_id={"depth": other // freqs, "freq": other % freqs},
            device_id_type=MESH,
        )
        return carry

    lax.fori_loop(1, depth * freqs, greet, 0)

    for small in smalls:
        small.wait()
    for f in range(freq_count):
        patches[f, 3 * MAIN + 3 * WINDOW :, :] = jnp.zeros((WINDOW, PARTS * width), jnp.bfloat16)
        step = column(phase_step[f : f + 1, :], kernels)
        shift = column(phase_shift[f : f + 1, :], kernels)
        weights = [column(stencil[j, f : f + 1, :], kernels) for j in range(5)]
        kern = build_taps(weights, step, shift, kernels)
        for c in range(2):
            for t in range(len(kern[c])):
                for y in range(ROWS):
                    moved = pltpu.roll(kern[c][t], y, 1) if y else kern[c][t]
                    spread[f, t, pl.ds(c * ROWS + y, kernels, stride=2 * ROWS), :] = moved
        for t in range(MAIN // LANES):
            high, low = split(spread[f, t])
            taps[f, :, t * LANES : (t + 1) * LANES] = high
            taps[f, :, MAIN + t * LANES : MAIN + (t + 1) * LANES] = high
            taps[f, :, 2 * MAIN + t * LANES : 2 * MAIN + (t + 1) * LANES] = low
        high, low = split(spread[f, MAIN // LANES])
        high, low = high.astype(jnp.float32), low.astype(jnp.float32)
        last = high + pltpu.roll(high, WINDOW, 1) + pltpu.roll(low, 2 * WINDOW, 1)
        taps[f, :, 3 * MAIN :] = last.astype(jnp.bfloat16)

    own_bins.wait()
    for c in range(2):
        load_copy(c, 0).wait()
        pl.when(has_up)(load_copy(c, 1).wait)
        pl.when(has_down)(load_copy(c, 2).wait)
    pl.semaphore_wait(barrier, depth * freqs - 1)

    def bins_copy(target, level, sem):
        rows = pl.ds(pl.multiple_of(snake(target % strips) * ROWS, ROWS), ROWS)
        return pltpu.make_async_remote_copy(
            src_ref=bins.at[0, rows, :], dst_ref=level_bins.at[level],
            send_sem=bins_send.at[sem], recv_sem=bins_recv.at[level],
            device_id={"depth": target}, device_id_type=MESH,
        )

    def send_bins(step, carry):
        bins_copy((here + step) % depth, here, step).start()
        return carry

    lax.fori_loop(1, depth, send_bins, 0)

    up = group * strips + snake(jnp.maximum(strip - 1, 0))
    down = group * strips + snake(jnp.minimum(strip + 1, strips - 1))

    def halo_copy(slot, f, way):
        source = HALO if way == 0 else ROWS
        target = HALO + ROWS if way == 0 else 0
        return pltpu.make_async_remote_copy(
            src_ref=field.at[slot, f, :, :, pl.ds(source, HALO), :],
            dst_ref=field.at[slot, f, :, :, pl.ds(target, HALO), :],
            send_sem=halo_send.at[way, slot, f], recv_sem=halo_recv.at[way, slot, f],
            device_id={"depth": up if way == 0 else down}, device_id_type=MESH,
        )

    def swap_copy(index):
        return pltpu.make_async_remote_copy(
            src_ref=part.at[index, pl.ds((1 - core) * share, share)], dst_ref=mirror.at[index],
            send_sem=swap_send.at[index], recv_sem=swap_recv.at[index],
            device_id={"freq": 1 - core}, device_id_type=MESH,
        )

    out_core = strip // per_core

    def out_copy(index, from_core, from_place):
        rows = pl.ds(pl.multiple_of(from_place * ROWS, ROWS), ROWS)
        return pltpu.make_async_remote_copy(
            src_ref=total.at[index], dst_ref=out.at[pl.ds(from_core * share, share), rows, :],
            send_sem=out_send.at[index], recv_sem=out_recv.at[from_core, from_place],
            device_id={"depth": group * strips + index, "freq": out_core}, device_id_type=MESH,
        )

    def owned(index):
        return (group * strips + index == here) & (out_core == core)

    def collect(index):
        swap_copy(index).wait()
        total[index] = part[index, pl.ds(core * share, share)] + mirror[index]

    def deliver(index):
        @pl.when(owned(index))
        def _():
            rows = pl.ds(pl.multiple_of(strip % per_core * ROWS, ROWS), ROWS)
            out[pl.ds(core * share, share), rows, :] = total[index]

        @pl.when(jnp.logical_not(owned(index)))
        def _():
            out_copy(index, core, strip % per_core).start()

    def deliver_early(step, carry):
        index = (strip + step) % strips
        pl.when(index < strips - 1)(lambda: deliver(index))
        return carry

    wide = lax.broadcasted_iota(jnp.int32, (WINDOW, width), 1)
    lane = lax.broadcasted_iota(jnp.int32, (ROWS, width), 1)

    def level(z, carry):
        slot = z % 2
        after = 1 - slot
        index = z - group * strips

        for f in range(freq_count):
            for way, has_send, has_recv in ((0, has_up, has_down), (1, has_down, has_up)):

                @pl.when((z > 0) & has_recv)
                def _():
                    halo_copy(slot, f, way).wait_recv()

                @pl.when((z > 0) & has_send)
                def _():
                    halo_copy(slot, f, way).wait_send()

            if f == freq_count - 1:
                pl.when((index >= 1) & (index <= strips))(lambda: collect(index - 1))

                @pl.when(index == strips - 1)
                def _():
                    lax.fori_loop(1, strips + 1, deliver_early, 0)

                pl.when(index == strips)(lambda: deliver(strips - 1))

            for j in range(PARTS):
                halves = split(field[slot, f, j // 2, j % 2])
                cols = slice(j * width, (j + 1) * width)
                for b in range(TAPS):
                    reach = b - HALF
                    high, low = halves
                    if reach:
                        inside = wide < width - reach if reach > 0 else wide >= -reach
                        high, low = (
                            jnp.where(inside, pltpu.roll(half, (-reach) % width, 1), jnp.zeros_like(half))
                            for half in halves
                        )
                    if b < TAPS - 1:
                        places = [b * WINDOW + n * MAIN for n in range(3)]
                    else:
                        places = [3 * MAIN + n * WINDOW for n in range(3)]
                    for place, piece in zip(places, (high, low, high)):
                        patches[f, place : place + WINDOW, cols] = piece
            result = jnp.dot(taps[f], patches[f], preferred_element_type=jnp.float32)

            if f == 0:

                @pl.when(z != here)
                def _():
                    bins_copy(here, z, 0).wait_recv()

            chosen = level_bins[z]
            picked = None
            for k in range(kernels):
                rows = [
                    [
                        result[
                            (2 * k + c) * ROWS : (2 * k + c + 1) * ROWS,
                            j * width : (j + 1) * width,
                        ]
                        for j in range(PARTS)
                    ]
                    for c in range(2)
                ]
                if picked is None:
                    picked = rows
                else:
                    mask = chosen == k
                    picked = [
                        [jnp.where(mask, rows[c][j], picked[c][j]) for j in range(PARTS)]
                        for c in range(2)
                    ]
            for pair in range(PARTS // 2):
                re, im = 2 * pair, 2 * pair + 1
                field[after, f, pair, 0, pl.ds(HALO, ROWS), :] = picked[0][re] - picked[1][im]
                field[after, f, pair, 1, pl.ds(HALO, ROWS), :] = picked[0][im] + picked[1][re]

            for way, has_send in ((0, has_up), (1, has_down)):

                @pl.when((z < depth - 1) & has_send)
                def _():
                    halo_copy(after, f, way).start()

        @pl.when((index >= 0) & (index < strips))
        def _():
            for n in range(lag_count):
                lag = lags[n]
                back = lax.rem(width - 2 * lag, width)
                product = jnp.zeros((ROWS, width), jnp.float32)
                for f in range(freq_count):
                    for j in range(PARTS // 2):
                        source = field[after, f, 0, j, pl.ds(HALO, ROWS), :]
                        receiver = field[after, f, 1, j, pl.ds(HALO, ROWS), :]
                        product += source * pltpu.roll(receiver, back, 1)
                product = jnp.where(lane < width - 2 * lag, product, 0.0)
                part[index, n] = pltpu.roll(product, lag, 1)
            swap_copy(index).start()

        return carry

    lax.fori_loop(0, depth, level, 0)

    @pl.when(group == groups - 1)
    def _():
        collect(strips - 1)
        deliver(strips - 1)

    def finish_out(index, carry):
        @pl.when(jnp.logical_not(owned(index)))
        def _():
            out_copy(index, core, strip % per_core).wait_send()

        return carry

    def finish_bins(step, carry):
        bins_copy((here + step) % depth, here, step).wait_send()
        return carry

    for from_core in range(freqs):
        for place in range(per_core):
            sender = core * per_core + place

            @pl.when((sender != strip) | (core != from_core))
            def _():
                out_copy(0, from_core, place).wait_recv()

    lax.fori_loop(0, strips, finish_out, 0)
    lax.fori_loop(1, depth, finish_bins, 0)


def body(surface, bins, stencil, phase_step, phase_shift, lags, *, depth, freqs):
    freq_count = surface.shape[1]
    height = surface.shape[3]
    width = surface.shape[4] // 2
    kernels = stencil.shape[1]
    lag_count = lags.shape[0]
    strips = height // ROWS
    groups = depth // strips
    per_core = strips // freqs
    share = lag_count // freqs
    tiles = -(-TAPS // PER_TILE)
    cost = 2 * freq_count * depth * 2 * kernels * ROWS * CONTRACT * PARTS * width
    vmem = pl.BlockSpec(memory_space=pltpu.VMEM)
    image = pl.pallas_call(
        functools.partial(kernel, depth, groups, freqs),
        out_shape=jax.ShapeDtypeStruct((lag_count, per_core * ROWS, width), jnp.float32),
        in_specs=[pl.BlockSpec(memory_space=pl.ANY)] * 6,
        out_specs=vmem,
        scratch_shapes=[
            pltpu.VMEM((stencil.shape[2], freq_count, kernels), jnp.float32),
            pltpu.VMEM(phase_step.shape, jnp.float32),
            pltpu.VMEM(phase_shift.shape, jnp.float32),
            pltpu.SMEM(lags.shape, jnp.int32),
            pltpu.SemaphoreType.DMA((4,)),
            pltpu.VMEM((2, freq_count, PARTS // 2, 2, WINDOW, width), jnp.float32),
            pltpu.VMEM((depth, ROWS, width), jnp.int32),
            pltpu.VMEM((freq_count, tiles, 2 * kernels * ROWS, LANES), jnp.float32),
            pltpu.VMEM((freq_count, 2 * kernels * ROWS, CONTRACT), jnp.bfloat16),
            pltpu.VMEM((freq_count, CONTRACT, PARTS * width), jnp.bfloat16),
            pltpu.VMEM((strips, lag_count, ROWS, width), jnp.float32),
            pltpu.VMEM((strips, share, ROWS, width), jnp.float32),
            pltpu.VMEM((strips, share, ROWS, width), jnp.float32),
            pltpu.SemaphoreType.DMA((2, 3)),
            pltpu.SemaphoreType.DMA((depth,)),
            pltpu.SemaphoreType.DMA((depth,)),
            pltpu.SemaphoreType.DMA((2, 2, freq_count)),
            pltpu.SemaphoreType.DMA((2, 2, freq_count)),
            pltpu.SemaphoreType.DMA((strips,)),
            pltpu.SemaphoreType.DMA((strips,)),
            pltpu.SemaphoreType.DMA((strips,)),
            pltpu.SemaphoreType.DMA((freqs, per_core)),
        ],
        compiler_params=pltpu.CompilerParams(
            collective_id=0, has_side_effects=True, vmem_limit_bytes=60 * 1024 * 1024
        ),
        cost_estimate=pl.CostEstimate(flops=cost, bytes_accessed=1 << 20, transcendentals=0),
    )(surface, bins, jnp.transpose(stencil, (2, 0, 1)), phase_step, phase_shift, lags)
    return image.reshape(1, lag_count, per_core * ROWS * width)


def solution(mesh):
    return jax.shard_map(
        functools.partial(body, depth=mesh.shape["depth"], freqs=mesh.shape["freq"]),
        mesh=mesh,
        in_specs=(
            P("shots", "freq", None, None, None),
            P("depth", None, None),
            P("freq", None, None),
            P("freq", None),
            P("freq", None),
            P(),
        ),
        out_specs=P("depth", "shots", "freq"),
        check_vma=False,
    )
```

```python
import functools
import math

import jax
import jax.numpy as jnp
from jax import lax
from jax.experimental import pallas as pl
from jax.experimental.pallas import tpu as pltpu
from jax.sharding import PartitionSpec as P

HALF = 6
TAPS = 2 * HALF + 1
HALO = 8
ROWS = 16
WINDOW = ROWS + 2 * HALO
PARTS = 4
LANES = 128
PER_TILE = LANES // WINDOW
MAIN = (TAPS // PER_TILE) * LANES
CONTRACT = 3 * MAIN + LANES
MESH = pl.DeviceIdType.MESH


def snake(index):
    pair = index // 2
    return 2 * pair + (index % 2 + pair % 2) % 2


def column(row_values, count):
    rows = lax.broadcasted_iota(jnp.int32, (count, count), 0)
    cols = lax.broadcasted_iota(jnp.int32, (count, count), 1)
    spread = jnp.broadcast_to(row_values, (count, count))
    return jnp.sum(jnp.where(rows == cols, spread, 0.0), axis=1, keepdims=True)


def build_taps(weights, step, shift, kernels):
    center, along_x, along_y, main, anti = weights
    scale = step / (center + 2.0 * (along_x + along_y + main + anti))
    center, along_x, along_y, main, anti = (
        jnp.broadcast_to(part * scale, (kernels, LANES))
        for part in (center, along_x, along_y, main, anti)
    )
    lane = lax.broadcasted_iota(jnp.int32, (kernels, LANES), 1)
    tiles = -(-TAPS // PER_TILE)
    zero = jnp.zeros((kernels, LANES), jnp.float32)
    power = [zero for _ in range(tiles)]
    spot = (HALF % PER_TILE) * WINDOW + HALO
    power[HALF // PER_TILE] = jnp.where(lane == spot, 1.0, 0.0)
    real = list(power)
    imag = [zero for _ in range(tiles)]
    for order in range(1, HALF + 1):
        right = [pltpu.roll(tile, WINDOW, 1) for tile in power]
        left = [pltpu.roll(tile, LANES - WINDOW, 1) for tile in power]
        grown = []
        for t in range(tiles):
            before = jnp.where(lane < WINDOW, right[t - 1] if t else zero, right[t])
            after = jnp.where(
                lane >= LANES - WINDOW, left[t + 1] if t + 1 < tiles else zero, left[t]
            )
            tall = along_y * power[t]
            down = tall + main * before + anti * after
            up = tall + main * after + anti * before
            flat = center * power[t] + along_x * (before + after)
            grown.append(flat + pltpu.roll(down, 1, 1) + pltpu.roll(up, LANES - 1, 1))
        power = grown
        sign = 1.0 if order % 4 < 2 else -1.0
        factor = sign / math.factorial(order)
        target = imag if order % 2 else real
        for t in range(tiles):
            target[t] = target[t] + power[t] * factor
    cosine = jnp.broadcast_to(jnp.cos(shift), (kernels, LANES))
    sine = jnp.broadcast_to(jnp.sin(shift), (kernels, LANES))
    kern_real = [cosine * r - sine * i for r, i in zip(real, imag)]
    kern_imag = [sine * r + cosine * i for r, i in zip(real, imag)]
    return kern_real, kern_imag


def split(value):
    high = value.astype(jnp.bfloat16)
    low = (value - high.astype(jnp.float32)).astype(jnp.bfloat16)
    return high, low


def kernel(
    depth, groups, freqs,
    surface, bins, stencil_far, phase_step_far, phase_shift_far, lags_far, out,
    stencil, phase_step, phase_shift, lags, small_sem,
    field, middle, level_bins, spread, taps, patches, part, mirror, total,
    load_sem, bins_send, bins_recv, halo_send, halo_recv, swap_send, swap_recv, out_send, out_recv,
):
    freq_count = surface.shape[1]
    kernels = stencil.shape[2]
    width = surface.shape[4] // 2
    lag_count = lags.shape[0]
    strips = depth // groups
    share = lag_count // freqs
    per_core = strips // freqs
    here = lax.axis_index("depth")
    core = lax.axis_index("freq")
    group = here // strips
    strip = snake(here % strips)
    has_up = strip > 0
    has_down = strip < strips - 1

    field[...] = jnp.zeros_like(field)
    level_bins[...] = jnp.full(level_bins.shape, -1, jnp.int32)
    first = pl.multiple_of(strip * ROWS, ROWS)

    def load_copy(c, place):
        rows = (first, jnp.maximum(first - ROWS, 0), jnp.minimum(first + ROWS, (strips - 1) * ROWS))
        target = (ROWS, 0, 2 * ROWS)[place]
        return pltpu.make_async_copy(
            surface.at[0, :, :, pl.ds(pl.multiple_of(rows[place], ROWS), ROWS), pl.ds(c * width, width)],
            field.at[0, :, :, c, pl.ds(target, ROWS), :],
            load_sem.at[c, place],
        )

    def bins_places(target, level):
        owner = snake(target % strips) * ROWS
        start = jnp.clip(owner - HALO, 0, strips * ROWS - WINDOW)
        source = pl.ds(pl.multiple_of(start, HALO), WINDOW)
        place = pl.ds(pl.multiple_of(start - owner + ROWS, HALO), WINDOW)
        return bins.at[0, source, :], level_bins.at[level, place, :]

    smalls = [
        pltpu.make_async_copy(far, near, small_sem.at[n])
        for n, (far, near) in enumerate((
            (stencil_far, stencil), (phase_step_far, phase_step),
            (phase_shift_far, phase_shift), (lags_far, lags),
        ))
    ]
    for small in smalls:
        small.start()
    own_bins = pltpu.make_async_copy(*bins_places(here, here), bins_send.at[0])
    own_bins.start()
    for c in range(2):
        load_copy(c, 0).start()
        pl.when(has_up)(load_copy(c, 1).start)
        pl.when(has_down)(load_copy(c, 2).start)

    barrier = pltpu.get_barrier_semaphore()

    def greet(step, carry):
        other = (here * freqs + core + step) % (depth * freqs)
        pl.semaphore_signal(
            barrier, inc=1, device_id={"depth": other // freqs, "freq": other % freqs},
            device_id_type=MESH,
        )
        return carry

    lax.fori_loop(1, depth * freqs, greet, 0)

    for small in smalls:
        small.wait()
    for f in range(freq_count):
        patches[f, 3 * MAIN + 3 * WINDOW :, :] = jnp.zeros((WINDOW, 2 * PARTS * width), jnp.bfloat16)
        step = column(phase_step[f : f + 1, :], kernels)
        shift = column(phase_shift[f : f + 1, :], kernels)
        weights = [column(stencil[j, f : f + 1, :], kernels) for j in range(5)]
        kern = build_taps(weights, step, shift, kernels)
        for c in range(2):
            for t in range(len(kern[c])):
                for y in range(ROWS):
                    moved = pltpu.roll(kern[c][t], y, 1) if y else kern[c][t]
                    spread[f, t, pl.ds(c * ROWS + y, kernels, stride=2 * ROWS), :] = moved
        for t in range(MAIN // LANES):
            high, low = split(spread[f, t])
            taps[f, :, t * LANES : (t + 1) * LANES] = high
            taps[f, :, MAIN + t * LANES : MAIN + (t + 1) * LANES] = high
            taps[f, :, 2 * MAIN + t * LANES : 2 * MAIN + (t + 1) * LANES] = low
        high, low = split(spread[f, MAIN // LANES])
        high, low = high.astype(jnp.float32), low.astype(jnp.float32)
        last = high + pltpu.roll(high, WINDOW, 1) + pltpu.roll(low, 2 * WINDOW, 1)
        taps[f, :, 3 * MAIN :] = last.astype(jnp.bfloat16)

    own_bins.wait()
    for c in range(2):
        load_copy(c, 0).wait()
        pl.when(has_up)(load_copy(c, 1).wait)
        pl.when(has_down)(load_copy(c, 2).wait)
    pl.semaphore_wait(barrier, depth * freqs - 1)

    def bins_copy(target, level, sem):
        source, place = bins_places(target, level)
        return pltpu.make_async_remote_copy(
            src_ref=source, dst_ref=place,
            send_sem=bins_send.at[sem], recv_sem=bins_recv.at[level],
            device_id={"depth": target}, device_id_type=MESH,
        )

    def send_bins(step, carry):
        bins_copy((here + step) % depth, here, step).start()
        return carry

    lax.fori_loop(1, depth, send_bins, 0)

    up = group * strips + snake(jnp.maximum(strip - 1, 0))
    down = group * strips + snake(jnp.minimum(strip + 1, strips - 1))

    def halo_copy(slot, f, way):
        target = 2 * ROWS if way == 0 else 0
        return pltpu.make_async_remote_copy(
            src_ref=field.at[slot, f, :, :, pl.ds(ROWS, ROWS), :],
            dst_ref=field.at[slot, f, :, :, pl.ds(target, ROWS), :],
            send_sem=halo_send.at[way, slot, f], recv_sem=halo_recv.at[way, slot, f],
            device_id={"depth": up if way == 0 else down}, device_id_type=MESH,
        )

    def swap_copy(index):
        return pltpu.make_async_remote_copy(
            src_ref=part.at[index, pl.ds((1 - core) * share, share)], dst_ref=mirror.at[index],
            send_sem=swap_send.at[index], recv_sem=swap_recv.at[index],
            device_id={"freq": 1 - core}, device_id_type=MESH,
        )

    out_core = strip // per_core

    def out_copy(index, from_core, from_place):
        rows = pl.ds(pl.multiple_of(from_place * ROWS, ROWS), ROWS)
        return pltpu.make_async_remote_copy(
            src_ref=total.at[index], dst_ref=out.at[pl.ds(from_core * share, share), rows, :],
            send_sem=out_send.at[index], recv_sem=out_recv.at[from_core, from_place],
            device_id={"depth": group * strips + index, "freq": out_core}, device_id_type=MESH,
        )

    def owned(index):
        return (group * strips + index == here) & (out_core == core)

    def collect(index):
        swap_copy(index).wait()
        total[index] = part[index, pl.ds(core * share, share)] + mirror[index]

    def deliver(index):
        @pl.when(owned(index))
        def _():
            rows = pl.ds(pl.multiple_of(strip % per_core * ROWS, ROWS), ROWS)
            out[pl.ds(core * share, share), rows, :] = total[index]

        @pl.when(jnp.logical_not(owned(index)))
        def _():
            out_copy(index, core, strip % per_core).start()

    def deliver_early(step, carry):
        index = (strip + step) % strips
        pl.when(index < strips - 2)(lambda: deliver(index))
        return carry

    lane = lax.broadcasted_iota(jnp.int32, (ROWS, width), 1)

    def apply(f, values, choice):
        count = len(choice)
        height = (count + 1) * ROWS
        wide = lax.broadcasted_iota(jnp.int32, (height, width), 1)
        for j in range(PARTS):
            halves = split(values[j])
            for b in range(TAPS):
                reach = b - HALF
                high, low = halves
                if reach:
                    inside = wide < width - reach if reach > 0 else wide >= -reach
                    high, low = (
                        jnp.where(inside, pltpu.roll(half, (-reach) % width, 1), jnp.zeros_like(half))
                        for half in halves
                    )
                if b < TAPS - 1:
                    places = [b * WINDOW + n * MAIN for n in range(3)]
                else:
                    places = [3 * MAIN + n * WINDOW for n in range(3)]
                for n in range(count):
                    cols = slice((n * PARTS + j) * width, (n * PARTS + j + 1) * width)
                    for place, piece in zip(places, (high, low, high)):
                        patches[f, place : place + WINDOW, cols] = piece[n * ROWS : n * ROWS + WINDOW]
        result = jnp.dot(
            taps[f], patches[f, :, : count * PARTS * width], preferred_element_type=jnp.float32
        )
        outcome = []
        for n in range(count):
            picked = [[jnp.zeros((ROWS, width), jnp.float32)] * PARTS for _ in range(2)]
            for k in range(kernels):
                mask = choice[n] == k
                for c in range(2):
                    rows = slice((2 * k + c) * ROWS, (2 * k + c + 1) * ROWS)
                    picked[c] = [
                        jnp.where(
                            mask,
                            result[rows, (n * PARTS + j) * width : (n * PARTS + j + 1) * width],
                            picked[c][j],
                        )
                        for j in range(PARTS)
                    ]
            parts = []
            for re in range(0, PARTS, 2):
                parts.append(picked[0][re] - picked[1][re + 1])
                parts.append(picked[0][re + 1] + picked[1][re])
            outcome.append(parts)
        return outcome

    def correlate(index, read):
        for n in range(lag_count):
            lag = lags[n]
            back = lax.rem(width - 2 * lag, width)
            product = jnp.zeros((ROWS, width), jnp.float32)
            for f in range(freq_count):
                for j in range(2):
                    product += read(f, 0, j) * pltpu.roll(read(f, 1, j), back, 1)
            product = jnp.where(lane < width - 2 * lag, product, 0.0)
            part[index, n] = pltpu.roll(product, lag, 1)
        swap_copy(index).start()

    def two_levels(step, carry):
        z = 2 * step
        slot = step % 2
        after = 1 - slot
        index = z - group * strips

        for f in range(freq_count):
            for way, has_send, has_recv in ((0, has_up, has_down), (1, has_down, has_up)):

                @pl.when((step > 0) & has_recv)
                def _():
                    halo_copy(slot, f, way).wait_recv()

                @pl.when((step > 0) & has_send)
                def _():
                    halo_copy(slot, f, way).wait_send()

            if f == freq_count - 1:

                @pl.when((index >= 2) & (index <= strips))
                def _():
                    collect(index - 2)
                    collect(index - 1)

                @pl.when(index == strips - 2)
                def _():
                    lax.fori_loop(1, strips + 1, deliver_early, 0)

                @pl.when(index == strips)
                def _():
                    deliver(strips - 2)
                    deliver(strips - 1)

            if f == 0:
                for more in range(2):

                    @pl.when(z + more != here)
                    def _():
                        bins_copy(here, z + more, 0).wait_recv()

            choice = [
                level_bins[z, pl.ds(HALO, ROWS), :], level_bins[z, pl.ds(HALO + ROWS, ROWS), :]
            ]
            outcome = apply(f, [field[slot, f, j // 2, j % 2] for j in range(PARTS)], choice)
            for n in range(2):
                for j in range(PARTS):
                    middle[f, j // 2, j % 2, pl.ds(n * ROWS, ROWS), :] = outcome[n][j]
            choice = [level_bins[z + 1, pl.ds(ROWS, ROWS), :]]
            outcome = apply(f, [middle[f, j // 2, j % 2] for j in range(PARTS)], choice)
            for j in range(PARTS):
                field[after, f, j // 2, j % 2, pl.ds(ROWS, ROWS), :] = outcome[0][j]

            for way, has_send in ((0, has_up), (1, has_down)):

                @pl.when((z < depth - 2) & has_send)
                def _():
                    halo_copy(after, f, way).start()

        @pl.when((index >= 0) & (index < strips))
        def _():
            correlate(index, lambda f, pair, c: middle[f, pair, c, pl.ds(HALO, ROWS), :])
            correlate(index + 1, lambda f, pair, c: field[after, f, pair, c, pl.ds(ROWS, ROWS), :])

        return carry

    lax.fori_loop(0, depth // 2, two_levels, 0)

    @pl.when(group == groups - 1)
    def _():
        collect(strips - 2)
        deliver(strips - 2)
        collect(strips - 1)
        deliver(strips - 1)

    def finish_out(index, carry):
        @pl.when(jnp.logical_not(owned(index)))
        def _():
            out_copy(index, core, strip % per_core).wait_send()

        return carry

    def finish_bins(step, carry):
        bins_copy((here + step) % depth, here, step).wait_send()
        return carry

    for from_core in range(freqs):
        for place in range(per_core):
            sender = core * per_core + place

            @pl.when((sender != strip) | (core != from_core))
            def _():
                out_copy(0, from_core, place).wait_recv()

    lax.fori_loop(0, strips, finish_out, 0)
    lax.fori_loop(1, depth, finish_bins, 0)


def body(surface, bins, stencil, phase_step, phase_shift, lags, *, depth, freqs):
    freq_count = surface.shape[1]
    height = surface.shape[3]
    width = surface.shape[4] // 2
    kernels = stencil.shape[1]
    lag_count = lags.shape[0]
    strips = height // ROWS
    groups = depth // strips
    per_core = strips // freqs
    share = lag_count // freqs
    tiles = -(-TAPS // PER_TILE)
    cost = 2 * freq_count * depth * 2 * kernels * ROWS * CONTRACT * PARTS * width
    vmem = pl.BlockSpec(memory_space=pltpu.VMEM)
    image = pl.pallas_call(
        functools.partial(kernel, depth, groups, freqs),
        out_shape=jax.ShapeDtypeStruct((lag_count, per_core * ROWS, width), jnp.float32),
        in_specs=[pl.BlockSpec(memory_space=pl.ANY)] * 6,
        out_specs=vmem,
        scratch_shapes=[
            pltpu.VMEM((stencil.shape[2], freq_count, kernels), jnp.float32),
            pltpu.VMEM(phase_step.shape, jnp.float32),
            pltpu.VMEM(phase_shift.shape, jnp.float32),
            pltpu.SMEM(lags.shape, jnp.int32),
            pltpu.SemaphoreType.DMA((4,)),
            pltpu.VMEM((2, freq_count, PARTS // 2, 2, 3 * ROWS, width), jnp.float32),
            pltpu.VMEM((freq_count, PARTS // 2, 2, WINDOW, width), jnp.float32),
            pltpu.VMEM((depth, 3 * ROWS, width), jnp.int32),
            pltpu.VMEM((freq_count, tiles, 2 * kernels * ROWS, LANES), jnp.float32),
            pltpu.VMEM((freq_count, 2 * kernels * ROWS, CONTRACT), jnp.bfloat16),
            pltpu.VMEM((freq_count, CONTRACT, 2 * PARTS * width), jnp.bfloat16),
            pltpu.VMEM((strips, lag_count, ROWS, width), jnp.float32),
            pltpu.VMEM((strips, share, ROWS, width), jnp.float32),
            pltpu.VMEM((strips, share, ROWS, width), jnp.float32),
            pltpu.SemaphoreType.DMA((2, 3)),
            pltpu.SemaphoreType.DMA((depth,)),
            pltpu.SemaphoreType.DMA((depth,)),
            pltpu.SemaphoreType.DMA((2, 2, freq_count)),
            pltpu.SemaphoreType.DMA((2, 2, freq_count)),
            pltpu.SemaphoreType.DMA((strips,)),
            pltpu.SemaphoreType.DMA((strips,)),
            pltpu.SemaphoreType.DMA((strips,)),
            pltpu.SemaphoreType.DMA((freqs, per_core)),
        ],
        compiler_params=pltpu.CompilerParams(
            collective_id=0, has_side_effects=True, vmem_limit_bytes=60 * 1024 * 1024
        ),
        cost_estimate=pl.CostEstimate(flops=cost, bytes_accessed=1 << 20, transcendentals=0),
    )(surface, bins, jnp.transpose(stencil, (2, 0, 1)), phase_step, phase_shift, lags)
    return image.reshape(1, lag_count, per_core * ROWS * width)


def solution(mesh):
    return jax.shard_map(
        functools.partial(body, depth=mesh.shape["depth"], freqs=mesh.shape["freq"]),
        mesh=mesh,
        in_specs=(
            P("shots", "freq", None, None, None),
            P("depth", None, None),
            P("freq", None, None),
            P("freq", None),
            P("freq", None),
            P(),
        ),
        out_specs=P("depth", "shots", "freq"),
        check_vma=False,
    )
```

```python
import functools
import math

import jax
import jax.numpy as jnp
from jax import lax
from jax.experimental import pallas as pl
from jax.experimental.pallas import tpu as pltpu
from jax.sharding import PartitionSpec as P

HALF = 6
TAPS = 2 * HALF + 1
HALO = 8
ROWS = 16
WINDOW = ROWS + 2 * HALO
PARTS = 4
LANES = 128
PER_TILE = LANES // WINDOW
MAIN = (TAPS // PER_TILE) * LANES
CONTRACT = 3 * MAIN + LANES
MESH = pl.DeviceIdType.MESH


def snake(index):
    pair = index // 2
    return 2 * pair + (index % 2 + pair % 2) % 2


def build_taps(weights, step, shift, kernels):
    center, along_x, along_y, main, anti = weights
    scale = step / (center + 2.0 * (along_x + along_y + main + anti))
    center, along_x, along_y, main, anti = (
        part * scale for part in (center, along_x, along_y, main, anti)
    )
    lane = lax.broadcasted_iota(jnp.int32, (kernels, LANES), 1)
    tiles = -(-TAPS // PER_TILE)
    zero = jnp.zeros((kernels, LANES), jnp.float32)
    power = [zero for _ in range(tiles)]
    spot = (HALF % PER_TILE) * WINDOW + HALO
    power[HALF // PER_TILE] = jnp.where(lane == spot, 1.0, 0.0)
    real = list(power)
    imag = [zero for _ in range(tiles)]
    for order in range(1, HALF + 1):
        right = [pltpu.roll(tile, WINDOW, 1) for tile in power]
        left = [pltpu.roll(tile, LANES - WINDOW, 1) for tile in power]
        grown = []
        for t in range(tiles):
            before = jnp.where(lane < WINDOW, right[t - 1] if t else zero, right[t])
            after = jnp.where(
                lane >= LANES - WINDOW, left[t + 1] if t + 1 < tiles else zero, left[t]
            )
            tall = along_y * power[t]
            down = tall + main * before + anti * after
            up = tall + main * after + anti * before
            flat = center * power[t] + along_x * (before + after)
            grown.append(flat + pltpu.roll(down, 1, 1) + pltpu.roll(up, LANES - 1, 1))
        power = grown
        sign = 1.0 if order % 4 < 2 else -1.0
        factor = sign / math.factorial(order)
        target = imag if order % 2 else real
        for t in range(tiles):
            target[t] = target[t] + power[t] * factor
    cosine, sine = jnp.cos(shift), jnp.sin(shift)
    kern_real = [cosine * r - sine * i for r, i in zip(real, imag)]
    kern_imag = [sine * r + cosine * i for r, i in zip(real, imag)]
    return kern_real, kern_imag


def split(value):
    high = value.astype(jnp.bfloat16)
    low = (value - high.astype(jnp.float32)).astype(jnp.bfloat16)
    return high, low


def kernel(
    depth, groups, freqs,
    surface, bins, stencil_far, phase_step_far, phase_shift_far, lags_far, out,
    got, stencil, phase_step, phase_shift, lags, small_sem,
    field, middle, level_bins, spread, taps, patches, part, mirror, total,
    load_sem, bins_send, bins_recv, halo_send, halo_recv, swap_send, swap_recv, out_send, out_recv,
):
    freq_count = surface.shape[1]
    kernels = stencil.shape[2]
    width = surface.shape[4] // 2
    lag_count = lags.shape[0]
    strips = depth // groups
    share = lag_count // freqs
    per_core = strips // freqs
    here = lax.axis_index("depth")
    core = lax.axis_index("freq")
    group = here // strips
    strip = snake(here % strips)
    has_up = strip > 0
    has_down = strip < strips - 1

    field[...] = jnp.zeros_like(field)
    level_bins[...] = jnp.full(level_bins.shape, -1, jnp.int32)
    first = pl.multiple_of(strip * ROWS, ROWS)

    def load_copy(c, place):
        rows = (first, jnp.maximum(first - ROWS, 0), jnp.minimum(first + ROWS, (strips - 1) * ROWS))
        target = (ROWS, 0, 2 * ROWS)[place]
        return pltpu.make_async_copy(
            surface.at[0, :, :, pl.ds(pl.multiple_of(rows[place], ROWS), ROWS), pl.ds(c * width, width)],
            field.at[0, :, :, c, pl.ds(target, ROWS), :],
            load_sem.at[c, place],
        )

    def bins_places(target, level):
        owner = snake(target % strips) * ROWS
        start = jnp.clip(owner - HALO, 0, strips * ROWS - WINDOW)
        source = pl.ds(pl.multiple_of(start, HALO), WINDOW)
        place = pl.ds(pl.multiple_of(start - owner + ROWS, HALO), WINDOW)
        return bins.at[0, source, :], level_bins.at[level, place, :]

    smalls = [
        pltpu.make_async_copy(far, near, small_sem.at[n])
        for n, (far, near) in enumerate((
            (stencil_far, stencil), (phase_step_far, phase_step),
            (phase_shift_far, phase_shift), (lags_far, lags),
        ))
    ]
    for small in smalls:
        small.start()
    own_bins = pltpu.make_async_copy(*bins_places(here, here), bins_send.at[0])
    own_bins.start()
    for c in range(2):
        load_copy(c, 0).start()
        pl.when(has_up)(load_copy(c, 1).start)
        pl.when(has_down)(load_copy(c, 2).start)

    barrier = pltpu.get_barrier_semaphore()

    def greet(step, carry):
        other = (here * freqs + core + step) % (depth * freqs)
        pl.semaphore_signal(
            barrier, inc=1, device_id={"depth": other // freqs, "freq": other % freqs},
            device_id_type=MESH,
        )
        return carry

    lax.fori_loop(1, depth * freqs, greet, 0)

    for small in smalls:
        small.wait()
    def column(values):
        shape = (kernels, LANES)
        rows = lax.broadcasted_iota(jnp.int32, (kernels, kernels), 0)
        cols = lax.broadcasted_iota(jnp.int32, (kernels, kernels), 1)
        pieces = []
        for f in range(freq_count):
            wide = jnp.broadcast_to(values[f : f + 1, :], (kernels, kernels))
            narrow = jnp.sum(jnp.where(rows == cols, wide, 0.0), axis=1, keepdims=True)
            pieces.append(jnp.broadcast_to(narrow, shape))
        return jnp.concatenate(pieces, axis=0)

    kern = build_taps(
        [column(stencil[j]) for j in range(5)], column(phase_step[...]), column(phase_shift[...]),
        freq_count * kernels,
    )

    own_bins.wait()
    pl.semaphore_wait(barrier, depth * freqs - 1)

    def bins_copy(target, level, sem):
        source, place = bins_places(target, level)
        return pltpu.make_async_remote_copy(
            src_ref=source, dst_ref=place,
            send_sem=bins_send.at[sem], recv_sem=bins_recv.at[level],
            device_id={"depth": target}, device_id_type=MESH,
        )

    def send_bins(step, carry):
        bins_copy((here + step) % depth, here, step).start()
        return carry

    lax.fori_loop(1, depth, send_bins, 0)

    for f in range(freq_count):
        patches[f, 3 * MAIN + 3 * WINDOW :, :] = jnp.zeros((WINDOW, 2 * PARTS * width), jnp.bfloat16)
        for c in range(2):
            for t in range(len(kern[c])):
                for y in range(ROWS):
                    moved = kern[c][t][f * kernels : (f + 1) * kernels]
                    if y:
                        moved = pltpu.roll(moved, y, 1)
                    spread[f, t, pl.ds(c * ROWS + y, kernels, stride=2 * ROWS), :] = moved
        for t in range(MAIN // LANES):
            high, low = split(spread[f, t])
            taps[f, :, t * LANES : (t + 1) * LANES] = high
            taps[f, :, MAIN + t * LANES : MAIN + (t + 1) * LANES] = high
            taps[f, :, 2 * MAIN + t * LANES : 2 * MAIN + (t + 1) * LANES] = low
        high, low = split(spread[f, MAIN // LANES])
        high, low = high.astype(jnp.float32), low.astype(jnp.float32)
        last = high + pltpu.roll(high, WINDOW, 1) + pltpu.roll(low, 2 * WINDOW, 1)
        taps[f, :, 3 * MAIN :] = last.astype(jnp.bfloat16)

    for c in range(2):
        load_copy(c, 0).wait()
        pl.when(has_up)(load_copy(c, 1).wait)
        pl.when(has_down)(load_copy(c, 2).wait)

    up = group * strips + snake(jnp.maximum(strip - 1, 0))
    down = group * strips + snake(jnp.minimum(strip + 1, strips - 1))

    def halo_copy(slot, f, way):
        target = 2 * ROWS if way == 0 else 0
        return pltpu.make_async_remote_copy(
            src_ref=field.at[slot, f, :, :, pl.ds(ROWS, ROWS), :],
            dst_ref=field.at[slot, f, :, :, pl.ds(target, ROWS), :],
            send_sem=halo_send.at[way, slot, f], recv_sem=halo_recv.at[way, slot, f],
            device_id={"depth": up if way == 0 else down}, device_id_type=MESH,
        )

    def swap_copy(index):
        return pltpu.make_async_remote_copy(
            src_ref=part.at[index, pl.ds((1 - core) * share, share)], dst_ref=mirror.at[index],
            send_sem=swap_send.at[index], recv_sem=swap_recv.at[index],
            device_id={"freq": 1 - core}, device_id_type=MESH,
        )

    out_core = strip // per_core

    def out_copy(index, from_core, from_place):
        rows = pl.ds(pl.multiple_of(from_place * ROWS, ROWS), ROWS)
        return pltpu.make_async_remote_copy(
            src_ref=total.at[index], dst_ref=got.at[pl.ds(from_core * share, share), rows, :],
            send_sem=out_send.at[index], recv_sem=out_recv.at[from_core, from_place],
            device_id={"depth": group * strips + index, "freq": out_core}, device_id_type=MESH,
        )

    def owned(index):
        return (group * strips + index == here) & (out_core == core)

    def collect(index):
        swap_copy(index).wait()
        total[index] = part[index, pl.ds(core * share, share)] + mirror[index]

    def deliver(index):
        @pl.when(owned(index))
        def _():
            rows = pl.ds(pl.multiple_of(strip % per_core * ROWS, ROWS), ROWS)
            got[pl.ds(core * share, share), rows, :] = total[index]

        @pl.when(jnp.logical_not(owned(index)))
        def _():
            out_copy(index, core, strip % per_core).start()

    def deliver_early(step, carry):
        index = (strip + step) % strips
        pl.when(index < strips - 2)(lambda: deliver(index))
        return carry

    lane = lax.broadcasted_iota(jnp.int32, (ROWS, width), 1)

    def apply(f, values, z, places):
        count = len(places)
        height = (count + 1) * ROWS
        wide = lax.broadcasted_iota(jnp.int32, (height, width), 1)
        for j in range(PARTS):
            halves = split(values[j])
            for b in range(TAPS):
                reach = b - HALF
                high, low = halves
                if reach:
                    inside = wide < width - reach if reach > 0 else wide >= -reach
                    high, low = (
                        jnp.where(inside, pltpu.roll(half, (-reach) % width, 1), jnp.zeros_like(half))
                        for half in halves
                    )
                if b < TAPS - 1:
                    spots = [b * WINDOW + n * MAIN for n in range(3)]
                else:
                    spots = [3 * MAIN + n * WINDOW for n in range(3)]
                for n in range(count):
                    cols = slice((n * PARTS + j) * width, (n * PARTS + j + 1) * width)
                    for spot, piece in zip(spots, (high, low, high)):
                        patches[f, spot : spot + WINDOW, cols] = piece[n * ROWS : n * ROWS + WINDOW]
        result = jnp.dot(
            taps[f], patches[f, :, : count * PARTS * width], preferred_element_type=jnp.float32
        )
        if f == 0:

            @pl.when(z != here)
            def _():
                bins_copy(here, z, 0).wait_recv()

        choice = [level_bins[z, pl.ds(place, ROWS), :] for place in places]
        outcome = []
        for n in range(count):
            picked = [[jnp.zeros((ROWS, width), jnp.float32)] * PARTS for _ in range(2)]
            for k in range(kernels):
                mask = choice[n] == k
                for c in range(2):
                    rows = slice((2 * k + c) * ROWS, (2 * k + c + 1) * ROWS)
                    picked[c] = [
                        jnp.where(
                            mask,
                            result[rows, (n * PARTS + j) * width : (n * PARTS + j + 1) * width],
                            picked[c][j],
                        )
                        for j in range(PARTS)
                    ]
            parts = []
            for re in range(0, PARTS, 2):
                parts.append(picked[0][re] - picked[1][re + 1])
                parts.append(picked[0][re + 1] + picked[1][re])
            outcome.append(parts)
        return outcome

    def correlate(index, read):
        for n in range(lag_count):
            lag = lags[n]
            back = lax.rem(width - 2 * lag, width)
            product = jnp.zeros((ROWS, width), jnp.float32)
            for f in range(freq_count):
                for j in range(2):
                    product += read(f, 0, j) * pltpu.roll(read(f, 1, j), back, 1)
            product = jnp.where(lane < width - 2 * lag, product, 0.0)
            part[index, n] = pltpu.roll(product, lag, 1)
        swap_copy(index).start()

    def two_levels(step, carry):
        z = 2 * step
        slot = step % 2
        after = 1 - slot
        index = z - group * strips

        for f in range(freq_count):
            for way, has_send, has_recv in ((0, has_up, has_down), (1, has_down, has_up)):

                @pl.when((step > 0) & has_recv)
                def _():
                    halo_copy(slot, f, way).wait_recv()

                @pl.when((step > 0) & has_send)
                def _():
                    halo_copy(slot, f, way).wait_send()

            if f == freq_count - 1:

                @pl.when((index >= 2) & (index <= strips))
                def _():
                    collect(index - 2)
                    collect(index - 1)

                @pl.when(index == strips - 2)
                def _():
                    lax.fori_loop(1, strips + 1, deliver_early, 0)

                @pl.when(index == strips)
                def _():
                    deliver(strips - 2)
                    deliver(strips - 1)

            values = [field[slot, f, j // 2, j % 2] for j in range(PARTS)]
            outcome = apply(f, values, z, (HALO, HALO + ROWS))
            for n in range(2):
                for j in range(PARTS):
                    middle[f, j // 2, j % 2, pl.ds(n * ROWS, ROWS), :] = outcome[n][j]

            if f == freq_count - 1:

                @pl.when((index >= 0) & (index < strips))
                def _():
                    correlate(index, lambda g, pair, c: middle[g, pair, c, pl.ds(HALO, ROWS), :])

            values = [middle[f, j // 2, j % 2] for j in range(PARTS)]
            outcome = apply(f, values, z + 1, (ROWS,))
            for j in range(PARTS):
                field[after, f, j // 2, j % 2, pl.ds(ROWS, ROWS), :] = outcome[0][j]

            for way, has_send in ((0, has_up), (1, has_down)):

                @pl.when((z < depth - 2) & has_send)
                def _():
                    halo_copy(after, f, way).start()

        @pl.when((index >= 0) & (index < strips))
        def _():
            correlate(index + 1, lambda f, pair, c: field[after, f, pair, c, pl.ds(ROWS, ROWS), :])

        return carry

    lax.fori_loop(0, depth // 2, two_levels, 0)

    @pl.when(group == groups - 1)
    def _():
        collect(strips - 2)
        deliver(strips - 2)
        collect(strips - 1)
        deliver(strips - 1)

    def finish_out(index, carry):
        @pl.when(jnp.logical_not(owned(index)))
        def _():
            out_copy(index, core, strip % per_core).wait_send()

        return carry

    def finish_bins(step, carry):
        bins_copy((here + step) % depth, here, step).wait_send()
        return carry

    for from_core in range(freqs):
        for place in range(per_core):
            sender = core * per_core + place

            @pl.when((sender != strip) | (core != from_core))
            def _():
                out_copy(0, from_core, place).wait_recv()

    for row in range(per_core * ROWS):
        out[0, :, row * width : (row + 1) * width] = got[:, row, :]
    lax.fori_loop(0, strips, finish_out, 0)
    lax.fori_loop(1, depth, finish_bins, 0)


def body(surface, bins, stencil, phase_step, phase_shift, lags, *, depth, freqs):
    freq_count = surface.shape[1]
    height = surface.shape[3]
    width = surface.shape[4] // 2
    kernels = stencil.shape[1]
    lag_count = lags.shape[0]
    strips = height // ROWS
    groups = depth // strips
    per_core = strips // freqs
    share = lag_count // freqs
    tiles = -(-TAPS // PER_TILE)
    cost = 2 * freq_count * depth * 2 * kernels * ROWS * CONTRACT * PARTS * width
    vmem = pl.BlockSpec(memory_space=pltpu.VMEM)
    return pl.pallas_call(
        functools.partial(kernel, depth, groups, freqs),
        out_shape=jax.ShapeDtypeStruct((1, lag_count, per_core * ROWS * width), jnp.float32),
        in_specs=[pl.BlockSpec(memory_space=pl.ANY)] * 6,
        out_specs=vmem,
        scratch_shapes=[
            pltpu.VMEM((lag_count, per_core * ROWS, width), jnp.float32),
            pltpu.VMEM((stencil.shape[2], freq_count, kernels), jnp.float32),
            pltpu.VMEM(phase_step.shape, jnp.float32),
            pltpu.VMEM(phase_shift.shape, jnp.float32),
            pltpu.SMEM(lags.shape, jnp.int32),
            pltpu.SemaphoreType.DMA((4,)),
            pltpu.VMEM((2, freq_count, PARTS // 2, 2, 3 * ROWS, width), jnp.float32),
            pltpu.VMEM((freq_count, PARTS // 2, 2, WINDOW, width), jnp.float32),
            pltpu.VMEM((depth, 3 * ROWS, width), jnp.int32),
            pltpu.VMEM((freq_count, tiles, 2 * kernels * ROWS, LANES), jnp.float32),
            pltpu.VMEM((freq_count, 2 * kernels * ROWS, CONTRACT), jnp.bfloat16),
            pltpu.VMEM((freq_count, CONTRACT, 2 * PARTS * width), jnp.bfloat16),
            pltpu.VMEM((strips, lag_count, ROWS, width), jnp.float32),
            pltpu.VMEM((strips, share, ROWS, width), jnp.float32),
            pltpu.VMEM((strips, share, ROWS, width), jnp.float32),
            pltpu.SemaphoreType.DMA((2, 3)),
            pltpu.SemaphoreType.DMA((depth,)),
            pltpu.SemaphoreType.DMA((depth,)),
            pltpu.SemaphoreType.DMA((2, 2, freq_count)),
            pltpu.SemaphoreType.DMA((2, 2, freq_count)),
            pltpu.SemaphoreType.DMA((strips,)),
            pltpu.SemaphoreType.DMA((strips,)),
            pltpu.SemaphoreType.DMA((strips,)),
            pltpu.SemaphoreType.DMA((freqs, per_core)),
        ],
        compiler_params=pltpu.CompilerParams(
            collective_id=0, has_side_effects=True, vmem_limit_bytes=60 * 1024 * 1024
        ),
        cost_estimate=pl.CostEstimate(flops=cost, bytes_accessed=1 << 20, transcendentals=0),
    )(surface, bins, jnp.transpose(stencil, (2, 0, 1)), phase_step, phase_shift, lags)


def solution(mesh):
    return jax.shard_map(
        functools.partial(body, depth=mesh.shape["depth"], freqs=mesh.shape["freq"]),
        mesh=mesh,
        in_specs=(
            P("shots", "freq", None, None, None),
            P("depth", None, None),
            P("freq", None, None),
            P("freq", None),
            P("freq", None),
            P(),
        ),
        out_specs=P("depth", "shots", "freq"),
        check_vma=False,
    )
```
